512 devices in a mesh: row: 16 (over y, x), col: 32 (over z, core).
Axes of the slice: x: 4, y: 4, z: 16, core: 2. Of those that a mesh axis runs over, the one named last changes fastest.
Arguments:
- rhs_own: float32 [2, 2048, 512], P(None, 'row'), may hold values from -6 to 6
- inverse: bfloat16 [4096, 512], P('col'), as said below
- offdiag: bfloat16 [12288, 4096], P('row', 'col'), may hold values from -0.125 to 0.125
- pattern: int32 [8, 96], P(None, 'row'), may hold values from 0 to 9, as said below
- rhs_ext: float32 [16384, 512], P(('row', 'col')), may hold values from -6 to 6
Outputs:
- solution: bfloat16 [4096, 512], P('col')
- remainder: float32 [16384, 512], P(('row', 'col'))
The draws below stay inside these ranges and needn't reach their ends.
Inputs may be any that keep to these rules, and one draw needn't show every extreme that they name: `pattern`: within one supernode and row group the 6 slots are distinct; a slot l < 2 of row group r appears for supernode s only when window tile l * 16 + r belongs to a supernode after s. `inverse`: each block of 512 rows is lower triangular with a positive diagonal.
All inputs are finite; a program needn't handle non-finite values.
Results may differ from the reference program's by a relative error of at most 0.0065.
Values may be sent and summed in bfloat16 or wider, within the bound.
No kernel may reach another device: no remote copies, remote signals or barrier semaphores. Data moves between devices by JAX's collectives and lax.ppermute only.
A program may use at most 64 MiB of HBM per device.

```python
import math
import jax
import jax.numpy as jnp
import numpy as np

TILE = 128
TPS = 4
RHS = 512
EXT_DEV = 8
NZ_DEV = 6
SN = 512
GROUPS = 16
COLTILES = 32
SUPER = 8
OWN_DEV = 2


def draw_inverse(key, part):
    key = jax.random.fold_in(key, 5)
    key_off, key_diag = jax.random.split(key)
    total_rows = COLTILES * TILE
    row_pos = jnp.arange(total_rows)[:, None] % SN
    col_pos = jnp.arange(SN)[None, :]
    lower = jax.random.normal(key_off, (total_rows, SN), jnp.float32) * (0.5 / math.sqrt(SN))
    diagonal = jax.random.uniform(key_diag, (total_rows, SN), jnp.float32, 0.5, 1.5)
    filled = jnp.where(col_pos < row_pos, lower, jnp.where(col_pos == row_pos, diagonal, 0.0))
    return filled.astype(jnp.bfloat16)


def draw_pattern(key, part):
    key = jax.random.fold_in(key, 9)
    slot_total = OWN_DEV + EXT_DEV
    scores = jax.random.randint(key, (SUPER, GROUPS, slot_total), 0, 4096) * slot_total
    scores = scores + jnp.arange(slot_total, dtype=jnp.int32)[None, None, :]
    node_ids = jnp.arange(SUPER, dtype=jnp.int32)[:, None, None]
    group_ids = jnp.arange(GROUPS, dtype=jnp.int32)[None, :, None]
    slot_ids = jnp.arange(slot_total, dtype=jnp.int32)[None, None, :]
    window_tile = slot_ids * GROUPS + group_ids
    invalid = (slot_ids < OWN_DEV) & (window_tile // TPS <= node_ids)
    scores = scores + invalid.astype(jnp.int32) * (4096 * slot_total)
    chosen = jnp.argsort(scores, axis=-1, stable=True)[..., :NZ_DEV]
    return chosen.astype(jnp.int32).reshape(SUPER, GROUPS * NZ_DEV)


def steps_of(stream_key, shape, cuts, low, top_value):
    def one(position, blocks):
        heights = jax.random.uniform(jax.random.fold_in(jax.random.fold_in(stream_key, 6), position), (blocks,), jnp.float32, low / len(cuts), top_value / len(cuts))
        return jnp.repeat(jnp.exp(heights), shape[position] // blocks).reshape((-1,) + (1,) * (len(shape) - position - 1))

    gain = one(*cuts[0])
    for cut in cuts[1:]:
        gain = gain * one(*cut)
    return gain


def scatter_about(own_key, shape, scale, bound, shards=(), kind=jnp.bfloat16):
    array = scale * jax.random.normal(own_key, shape, jnp.float32)
    if shards:
        array = array * steps_of(own_key, shape, shards, -0.22, 0.18)
    return jnp.clip(array, -bound, bound).astype(kind)


def setup_inputs(seed: int = 0) -> dict:
    keys = jax.random.split(jax.random.key(seed), 6)
    rhs_own = scatter_about(keys[0], (OWN_DEV, GROUPS * TILE, RHS), 1.0, 6.0, ((1, 16),), jnp.float32)
    inverse = draw_inverse(jax.random.fold_in(keys[5], 71), 0)
    offdiag = scatter_about(keys[2], (GROUPS * NZ_DEV * TILE, COLTILES * TILE), (4 * SN) ** -0.5, 0.125, ((0, 16), (1, 32)))
    pattern = draw_pattern(jax.random.fold_in(keys[5], 71), 0)
    rhs_ext = scatter_about(keys[4], (GROUPS * EXT_DEV * TILE, RHS), 1.0, 6.0, ((0, 512),), jnp.float32)
    return dict(rhs_own=rhs_own, inverse=inverse, offdiag=offdiag, pattern=pattern, rhs_ext=rhs_ext)


def reference(rhs_own, inverse, offdiag, pattern, rhs_ext):
    window_rhs = rhs_own.reshape(OWN_DEV * GROUPS, TILE, RHS)
    slot_total = OWN_DEV + EXT_DEV
    updates = jnp.zeros((GROUPS, slot_total, TILE, RHS), jnp.float32)
    group_ids = jnp.repeat(jnp.arange(GROUPS, dtype=jnp.int32), NZ_DEV)
    solved_list = []
    for section in range(SUPER):
        tile_ids = np.arange(TPS) + section * TPS
        current = window_rhs[tile_ids] - updates[tile_ids % GROUPS, tile_ids // GROUPS]
        current_bf = current.reshape(SN, RHS).astype(jnp.bfloat16)
        block_inverse = inverse[section * SN:(section + 1) * SN]
        solved = jnp.dot(block_inverse, current_bf, preferred_element_type=jnp.float32).astype(jnp.bfloat16)
        solved_list.append(solved)
        columns = offdiag[:, section * SN:(section + 1) * SN]
        products = jnp.dot(columns, solved, preferred_element_type=jnp.float32)
        products = products.reshape(GROUPS * NZ_DEV, TILE, RHS)
        updates = updates.at[group_ids, pattern[section].astype(jnp.int32)].add(products)
    solution = jnp.concatenate(solved_list, axis=0)
    below = updates[:, OWN_DEV:].reshape(GROUPS * EXT_DEV * TILE, RHS)
    return solution, rhs_ext - below
```

```python
import jax
import jax.numpy as jnp
from jax import lax
from jax.experimental import pallas as pl
from jax.experimental.pallas import tpu as pltpu
from jax.sharding import PartitionSpec as P

AXES = ("row", "col")
NX, NY, NZ, NC = 4, 4, 16, 2
TILE = 128
SUPER = 8
TPS = 4
NZ_DEV = 6
OWN = 2
RHS = 512
RZ = RHS // NZ
KEEP = 14
CHUNK = KEEP + 1
HALF = 8
INV0 = NZ_DEV * TILE
BLOB = INV0 + TPS * TILE
F32 = jnp.float32
BF = jnp.bfloat16
VMEM = 60 * 1024 * 1024


def dev(y, x, z, k):
    return ((y % NY) * NX + x % NX) * (NZ * NC) + (z % NZ) * NC + k % NC


def every():
    for y in range(NY):
        for x in range(NX):
            for z in range(NZ):
                for k in range(NC):
                    yield y, x, z, k


def home(slot, y, z):
    if slot == 0:
        return y, z + KEEP - 2 * y
    if y == 3 and z >= 8:
        return 0, z
    if y == 2 and z >= 10:
        return 1, z
    return y, z


def balance_pairs():
    pairs = []
    for y, x, z, k in every():
        for slot in range(OWN):
            if z < 8 * slot + 2 * y:
                to = home(slot, y, z)
                if to != (y, z):
                    pairs.append((dev(y, x, z, k), dev(to[0], x, to[1], k)))
    return pairs


def ring_pairs(stage, step):
    pairs = []
    for y, x, z, k in every():
        along_x = (k == 0) == (stage == 0)
        to = dev(y, x + step, z, k) if along_x else dev(y + step, x, z, k)
        pairs.append((dev(y, x, z, k), to))
    return pairs


def swap_pairs():
    return [(dev(y, x, z, k), dev(y, x, z, 1 - k)) for y, x, z, k in every()]


def move(value, pairs):
    return lax.ppermute(value, AXES, pairs)


def nt(a, b):
    return lax.dot_general(a, b, (((1,), (1,)), ((), ())), preferred_element_type=F32)


def prep_kernel(meta, off, inv, rhs, blob, send, keep, btile, flat):
    blob[:INV0] = off[...]
    for j in range(TPS):
        blob[INV0 + j * TILE : INV0 + (j + 1) * TILE] = inv[:, j * TILE : (j + 1) * TILE]
    tiles = []
    for slot in range(OWN):
        tile = jnp.zeros((TILE, TILE), F32)
        for k in range(NZ_DEV):
            block = off[k * TILE : (k + 1) * TILE].astype(F32)
            tile = jnp.where(meta[k] == slot, block, tile)
        tiles.append(tile)
    keep[...] = tiles[1].astype(BF)
    send[...] = jnp.where(meta[6] == 0, tiles[0], tiles[1]).astype(BF)
    start = pl.multiple_of(meta[7], RZ)
    for slot in range(OWN):
        flat[...] = rhs[slot].T
        part = flat[pl.ds(start, RZ), :]
        high = part.astype(BF)
        btile[slot * 2 * RZ : slot * 2 * RZ + RZ] = high
        btile[slot * 2 * RZ + RZ : (slot + 1) * 2 * RZ] = (part - high.astype(F32)).astype(BF)


def prep(meta, off, inv, rhs):
    tile = jax.ShapeDtypeStruct((TILE, TILE), BF)
    vm = pl.BlockSpec(memory_space=pltpu.VMEM)
    return pl.pallas_call(
        prep_kernel,
        out_shape=(jax.ShapeDtypeStruct((BLOB, TILE), BF), tile, tile, tile),
        in_specs=[pl.BlockSpec(memory_space=pltpu.SMEM), vm, vm, vm],
        out_specs=(vm, vm, vm, vm),
        scratch_shapes=[pltpu.VMEM((RHS, TILE), F32)],
        compiler_params=pltpu.CompilerParams(vmem_limit_bytes=VMEM),
    )(meta, off, inv, rhs)


PIECES = ((0, 4), (4, 4), (8, 2), (10, 2), (12, 4))


def solve_kernel(meta, pattern, *refs):
    pieces = refs[:10]
    blobs, out, factor, blob, upd, ext, sol, sems, bsems = refs[10:]
    core = meta[32]
    copies = []
    for h in range(2):
        for p, (first, count) in enumerate(PIECES):
            copies.append(
                pltpu.make_async_copy(
                    pieces[h * 5 + p], factor.at[h, pl.ds(first, count)], sems.at[h * 5 + p]
                )
            )
    loads = [
        pltpu.make_async_copy(
            blobs.at[pl.ds(s * TPS, TPS)], blob.at[pl.ds(s * TPS, TPS)], bsems.at[s]
        )
        for s in range(SUPER)
    ]
    for c in copies:
        c.start()
    for c in loads:
        c.start()
    upd[...] = jnp.zeros_like(upd)
    ext[...] = jnp.zeros_like(ext)
    for c in copies:
        c.wait()

    def block(parity, y, x, place):
        return factor[parity ^ core, meta[parity * 16 + y * NX + x], place]

    def rhs_tile(t):
        slot, r = t // 16, t % 16
        where = jnp.where(core == 0, meta[r], meta[16 + r])
        base = slot * 2 * RZ
        high = factor[0, where, KEEP, base : base + RZ].astype(F32)
        low = factor[0, where, KEEP, base + RZ : base + 2 * RZ].astype(F32)
        return high + low

    for s in range(SUPER):
        loads[s].wait()
        current = jnp.concatenate(
            [(rhs_tile(t) - upd[t]).astype(BF) for t in range(s * TPS, (s + 1) * TPS)], axis=1
        )
        solved = []
        for i in range(TPS):
            c = s * TPS + i
            rows = jnp.concatenate(
                [blob[c, INV0 + j * TILE : INV0 + (j + 1) * TILE] for j in range(i + 1)], axis=1
            )
            x_i = nt(current[:, : (i + 1) * TILE], rows).astype(BF)
            sol[c] = x_i
            solved.append(x_i)
        x_s = jnp.concatenate(solved, axis=1)
        for t in range((s + 1) * TPS, SUPER * TPS):
            slot, y, x = t // 16, t % 16 // NX, t % NX
            parts = []
            for j in range(TPS):
                at_y, place = home(slot, y, 2 * s + j // 2)
                parts.append(block(j % 2, at_y, x, place))
            upd[t] += nt(x_s, jnp.concatenate(parts, axis=1))
        for k in range(NZ_DEV):
            row0 = pl.multiple_of(k * TILE + core * 32, 32)
            row1 = pl.multiple_of(k * TILE + core * 32 + 64, 32)
            tops = [blob[s * TPS + j, pl.ds(row0, 32)] for j in range(TPS)]
            lows = [blob[s * TPS + j, pl.ds(row1, 32)] for j in range(TPS)]
            rows = jnp.concatenate(
                [jnp.concatenate(tops, axis=1), jnp.concatenate(lows, axis=1)], axis=0
            )
            ext[pattern[s * NZ_DEV + k]] += nt(x_s, rows)
    for z in range(NZ):
        out[z, :RZ] = sol[2 * z + core]
        part = ext[OWN + z // 2][:, (z % 2) * 32 : (z % 2) * 32 + 32]
        high = part.astype(BF)
        low = (part - high.astype(F32)).astype(BF)
        out[z, RZ:] = jnp.concatenate(
            [high, low, jnp.zeros((RZ, TILE - 64), BF)], axis=1
        )


def solve(meta, pattern, pieces, blobs):
    sm = pl.BlockSpec(memory_space=pltpu.SMEM)
    hbm = pl.BlockSpec(memory_space=pl.ANY)
    return pl.pallas_call(
        solve_kernel,
        out_shape=jax.ShapeDtypeStruct((NZ, 2 * RZ, TILE), BF),
        in_specs=[sm, sm] + [hbm] * 11,
        out_specs=pl.BlockSpec(memory_space=pltpu.VMEM),
        scratch_shapes=[
            pltpu.VMEM((2, 16, CHUNK, TILE, TILE), BF),
            pltpu.VMEM((SUPER * TPS, BLOB, TILE), BF),
            pltpu.VMEM((SUPER * TPS, RZ, TILE), F32),
            pltpu.VMEM((10, RZ, 64), F32),
            pltpu.VMEM((SUPER * TPS, RZ, TILE), BF),
            pltpu.SemaphoreType.DMA((10,)),
            pltpu.SemaphoreType.DMA((SUPER,)),
        ],
        compiler_params=pltpu.CompilerParams(vmem_limit_bytes=VMEM),
    )(meta, pattern, *pieces, blobs)


def finish_kernel(got, rhs_ext, solution, remainder):
    x = jnp.concatenate([got[z, :RZ].astype(F32) for z in range(NZ)], axis=0)
    solution[...] = x.T.astype(BF)
    tail = jnp.concatenate([got[z, RZ:].astype(F32) for z in range(NZ)], axis=0).T
    remainder[...] = rhs_ext[...] - (tail[:32] + tail[32:64])


def finish(got, rhs_ext):
    return pl.pallas_call(
        finish_kernel,
        out_shape=(
            jax.ShapeDtypeStruct((TILE, RHS), BF),
            jax.ShapeDtypeStruct((32, RHS), F32),
        ),
        compiler_params=pltpu.CompilerParams(vmem_limit_bytes=VMEM),
    )(got, rhs_ext)


def local(rhs_own, inverse, offdiag, pattern, rhs_ext):
    row, col = lax.axis_index("row"), lax.axis_index("col")
    y, x, z, core = row // NX, row % NX, col // NC, col % NC
    groups = [[NC * i + k for i in range(NZ)] for k in range(NC)]
    mine = lax.dynamic_index_in_dim(pattern, col // TPS, 0, keepdims=False)
    sends_first = z < 2 * y
    meta = jnp.concatenate(
        [mine, jnp.stack([jnp.where(sends_first, 0, 1), z * RZ]).astype(jnp.int32)]
    )
    blob, send, keep, btile = prep(meta, offdiag, inverse, rhs_own)
    blobs = lax.all_gather(blob, "col")
    got = move(send, balance_pairs())
    gets = (z < KEEP) & (z >= jnp.where((y == 0) | (y == 3), 8, 10))
    one = jnp.where(gets, got, keep)
    line = lax.all_gather(one, "col", axis_index_groups=groups)
    chunk = jnp.concatenate([line[:KEEP], btile[None]], axis=0)

    right = move(chunk, ring_pairs(0, -1))
    left = move(chunk, ring_pairs(0, 1))
    far = jnp.concatenate(
        [move(right[:HALF], ring_pairs(0, -1)), move(left[HALF:], ring_pairs(0, 1))], axis=0
    )
    first = jnp.stack([chunk, right, far, left])
    right = move(first, ring_pairs(1, -1))
    left = move(first, ring_pairs(1, 1))
    far_a = move(right[:2], ring_pairs(1, -1))
    far_b = move(left[2:], ring_pairs(1, 1))
    pieces = [first, right, far_a, far_b, left]
    pieces += [move(p, swap_pairs()) for p in pieces]

    places = []
    for parity in range(2):
        for r in range(16):
            dy, dx = (r // NX - y) % NY, (r % NX - x) % NX
            places.append(dy * 4 + dx if parity == 0 else dx * 4 + dy)
    table = jnp.stack(places + [core]).astype(jnp.int32)
    packed = solve(table, pattern.reshape(-1), pieces, blobs)
    home_again = lax.all_to_all(packed, "col", 0, 0, tiled=True, axis_index_groups=groups)
    return finish(home_again, rhs_ext)


def solution(mesh):
    return jax.shard_map(
        local,
        mesh=mesh,
        in_specs=(
            P(None, "row", None),
            P("col", None),
            P("row", "col"),
            P(None, "row"),
            P(("row", "col"), None),
        ),
        out_specs=(P("col", None), P(("row", "col"), None)),
        check_vma=False,
    )
```

```python
import jax
import jax.numpy as jnp
from jax import lax
from jax.experimental import pallas as pl
from jax.experimental.pallas import tpu as pltpu
from jax.sharding import PartitionSpec as P

AXES = ("row", "col")
NX, NY, NZ, NC = 4, 4, 16, 2
TILE = 128
SUPER = 8
TPS = 4
NZ_DEV = 6
OWN = 2
RHS = 512
RZ = RHS // NZ
KEEP = 14
CHUNK = KEEP + 1
EARLY = 11
RHS_AT = 10
INV0 = NZ_DEV * TILE
BLOB = INV0 + TPS * TILE
BLOCKS = NZ_DEV + TPS
F32 = jnp.float32
BF = jnp.bfloat16
VMEM = 60 * 1024 * 1024


def dev(y, x, z, k):
    return ((y % NY) * NX + x % NX) * (NZ * NC) + (z % NZ) * NC + k % NC


def every():
    for y in range(NY):
        for x in range(NX):
            for z in range(NZ):
                for k in range(NC):
                    yield y, x, z, k


def home(slot, y, z):
    if slot == 0:
        return y, z + KEEP - 2 * y
    if y == 3 and z >= 8:
        return 0, z
    if y == 2 and z >= 10:
        return 1, z
    return y, z


def place_of(z):
    if z < 4:
        return z
    return z + 7 if z < 8 else z - 4


def balance_pairs():
    pairs = []
    for y, x, z, k in every():
        for slot in range(OWN):
            if z < 8 * slot + 2 * y:
                to = home(slot, y, z)
                if to != (y, z):
                    pairs.append((dev(y, x, z, k), dev(to[0], x, to[1], k)))
    return pairs


def first_groups():
    groups = []
    for z in range(NZ):
        for k in range(NC):
            for a in range(4):
                groups.append([dev(a, b, z, k) if k == 0 else dev(b, a, z, k) for b in range(4)])
    return groups


def ring_pairs(step):
    return [
        (dev(y, x, z, k), dev(y + step, x, z, k) if k == 0 else dev(y, x + step, z, k))
        for y, x, z, k in every()
    ]


def swap_pairs():
    return [(dev(y, x, z, k), dev(y, x, z, 1 - k)) for y, x, z, k in every()]


def move(value, pairs):
    return lax.ppermute(value, AXES, pairs)


def nt(a, b):
    return lax.dot_general(a, b, (((1,), (1,)), ((), ())), preferred_element_type=F32)


def coordinates():
    row, col = lax.axis_index("row"), lax.axis_index("col")
    return row >> 2, row & 3, col >> 1, col & 1


def prep_kernel(pattern, off, inv, rhs, blob, send, keep, btile, flat):
    y, _, z, _ = coordinates()
    blob[:INV0] = off[...]
    for j in range(TPS):
        blob[INV0 + j * TILE : INV0 + (j + 1) * TILE] = inv[:, j * TILE : (j + 1) * TILE]
    tiles = []
    for slot in range(OWN):
        tile = jnp.zeros((TILE, TILE), F32)
        for k in range(NZ_DEV):
            block = off[k * TILE : (k + 1) * TILE].astype(F32)
            tile = jnp.where(pattern[z >> 1, k] == slot, block, tile)
        tiles.append(tile)
    keep[...] = tiles[1].astype(BF)
    send[...] = jnp.where(z < 2 * y, tiles[0], tiles[1]).astype(BF)
    start = pl.multiple_of(z * RZ, RZ)
    for slot in range(OWN):
        flat[...] = rhs[slot].T
        part = flat[pl.ds(start, RZ), :]
        high = part.astype(BF)
        btile[slot * 2 * RZ : slot * 2 * RZ + RZ] = high
        btile[slot * 2 * RZ + RZ : (slot + 1) * 2 * RZ] = (part - high.astype(F32)).astype(BF)


def prep(pattern, off, inv, rhs):
    tile = jax.ShapeDtypeStruct((TILE, TILE), BF)
    vm = pl.BlockSpec(memory_space=pltpu.VMEM)
    return pl.pallas_call(
        prep_kernel,
        out_shape=(jax.ShapeDtypeStruct((BLOB, TILE), BF), tile, tile, tile),
        in_specs=[pl.BlockSpec(memory_space=pltpu.SMEM), vm, vm, vm],
        out_specs=(vm, vm, vm, vm),
        scratch_shapes=[pltpu.VMEM((RHS, TILE), F32)],
        compiler_params=pltpu.CompilerParams(vmem_limit_bytes=VMEM),
    )(pattern, off, inv, rhs)


PIECES = ((0, 4), (4, 4), (8, 2), (10, 2), (12, 4))


def solve_kernel(pattern, *refs):
    pieces = refs[:10]
    blobs, out, factor, invs, rows_ext, upd, ext, sol, early, late, isems, esems = refs[10:]
    my_y, my_x, _, core = coordinates()

    def load(first, count, sems):
        return [
            pltpu.make_async_copy(
                pieces[h * 5 + p].at[:, pl.ds(first, count)],
                factor.at[h, pl.ds(at, blocks), pl.ds(first, count)],
                sems.at[h * 5 + p],
            )
            for h in range(2)
            for p, (at, blocks) in enumerate(PIECES)
        ]

    first_loads = load(0, EARLY, early)
    last_loads = load(EARLY, CHUNK - EARLY, late)
    inv_loads, ext_loads = [], []
    for s in range(SUPER):
        four = pl.ds(s * TPS, TPS)
        inv_loads.append(
            pltpu.make_async_copy(
                blobs.at[four, pl.ds(NZ_DEV, TPS)], invs.at[four], isems.at[s]
            )
        )
        ext_loads.append(
            pltpu.make_async_copy(
                blobs.at[four, pl.ds(0, NZ_DEV), :, core], rows_ext.at[four], esems.at[s]
            )
        )
    for c in first_loads[:5] + inv_loads[:1] + first_loads[5:] + inv_loads[1:2] + last_loads:
        c.start()
    for c in inv_loads[2:] + ext_loads:
        c.start()
    upd[...] = jnp.zeros_like(upd)
    ext[...] = jnp.zeros_like(ext)
    for c in first_loads:
        c.wait()

    def position(parity, y, x):
        if parity == 0:
            return ((y - my_y) & 3) * 4 + x
        return ((x - my_x) & 3) * 4 + y

    def block(parity, y, x, place):
        return factor[parity ^ core, position(parity, y, x), place]

    def rhs_tile(t):
        slot, y, x = t // 16, t % 16 // NX, t % NX
        where = jnp.where(core == 0, position(0, y, x), position(1, y, x))
        base = slot * 2 * RZ
        high = factor[0, where, RHS_AT, base : base + RZ].astype(F32)
        low = factor[0, where, RHS_AT, base + RZ : base + 2 * RZ].astype(F32)
        return high + low

    for s in range(SUPER):
        inv_loads[s].wait()
        if s == 2:
            for c in last_loads:
                c.wait()
        current = jnp.concatenate(
            [(rhs_tile(t) - upd[t]).astype(BF) for t in range(s * TPS, (s + 1) * TPS)], axis=1
        )
        solved = []
        for i in range(TPS):
            c = s * TPS + i
            rows = jnp.concatenate(
                [invs[c, j].reshape(TILE, TILE) for j in range(i + 1)], axis=1
            )
            x_i = nt(current[:, : (i + 1) * TILE], rows).astype(BF)
            sol[c] = x_i
            solved.append(x_i)
        x_s = jnp.concatenate(solved, axis=1)
        for t in range((s + 1) * TPS, SUPER * TPS):
            slot, y, x = t // 16, t % 16 // NX, t % NX
            parts = []
            for j in range(TPS):
                at_y, plane = home(slot, y, 2 * s + j // 2)
                parts.append(block(j % 2, at_y, x, place_of(plane)))
            upd[t] += nt(x_s, jnp.concatenate(parts, axis=1))
    for s in range(SUPER):
        ext_loads[s].wait()
        x_s = jnp.concatenate([sol[s * TPS + j] for j in range(TPS)], axis=1)
        for k in range(NZ_DEV):
            rows = jnp.concatenate(
                [rows_ext[s * TPS + j, k].reshape(64, TILE) for j in range(TPS)], axis=1
            )
            ext[pattern[s, k]] += nt(x_s, rows)
    for z in range(NZ):
        out[z, :RZ] = sol[2 * z + core]
        part = ext[OWN + z // 2][:, (z % 2) * 32 : (z % 2) * 32 + 32]
        high = part.astype(BF)
        low = (part - high.astype(F32)).astype(BF)
        out[z, RZ:] = jnp.concatenate(
            [high, low, jnp.zeros((RZ, TILE - 64), BF)], axis=1
        )


def solve(pattern, pieces, blobs):
    hbm = pl.BlockSpec(memory_space=pl.ANY)
    return pl.pallas_call(
        solve_kernel,
        out_shape=jax.ShapeDtypeStruct((NZ, 2 * RZ, TILE), BF),
        in_specs=[pl.BlockSpec(memory_space=pltpu.SMEM)] + [hbm] * 11,
        out_specs=pl.BlockSpec(memory_space=pltpu.VMEM),
        scratch_shapes=[
            pltpu.VMEM((2, 16, CHUNK, TILE, TILE), BF),
            pltpu.VMEM((SUPER * TPS, TPS, 2, 2, 32, TILE), BF),
            pltpu.VMEM((SUPER * TPS, NZ_DEV, 2, 32, TILE), BF),
            pltpu.VMEM((SUPER * TPS, RZ, TILE), F32),
            pltpu.VMEM((10, RZ, 64), F32),
            pltpu.VMEM((SUPER * TPS, RZ, TILE), BF),
            pltpu.SemaphoreType.DMA((10,)),
            pltpu.SemaphoreType.DMA((10,)),
            pltpu.SemaphoreType.DMA((SUPER,)),
            pltpu.SemaphoreType.DMA((SUPER,)),
        ],
        compiler_params=pltpu.CompilerParams(vmem_limit_bytes=VMEM),
    )(pattern, *pieces, blobs)


def finish_kernel(got, rhs_ext, solution, remainder):
    x = jnp.concatenate([got[z, :RZ].astype(F32) for z in range(NZ)], axis=0)
    solution[...] = x.T.astype(BF)
    tail = jnp.concatenate([got[z, RZ:].astype(F32) for z in range(NZ)], axis=0).T
    remainder[...] = rhs_ext[...] - (tail[:32] + tail[32:64])


def finish(got, rhs_ext):
    return pl.pallas_call(
        finish_kernel,
        out_shape=(
            jax.ShapeDtypeStruct((TILE, RHS), BF),
            jax.ShapeDtypeStruct((32, RHS), F32),
        ),
        compiler_params=pltpu.CompilerParams(vmem_limit_bytes=VMEM),
    )(got, rhs_ext)


def local(rhs_own, inverse, offdiag, pattern, rhs_ext):
    y, _, z, _ = coordinates()
    groups = [[NC * i + k for i in range(NZ)] for k in range(NC)]
    blob, send, keep, btile = prep(pattern, offdiag, inverse, rhs_own)
    blobs = lax.all_gather(blob, "col")
    got = move(send, balance_pairs())
    gets = (z < KEEP) & (z >= jnp.where((y == 0) | (y == 3), 8, 10))
    one = jnp.where(gets, got, keep)
    line = lax.all_gather(one, "col", axis_index_groups=groups)
    chunk = jnp.concatenate([line[:4], line[8:KEEP], btile[None], line[4:8]], axis=0)
    four = jnp.broadcast_to(chunk[None], (4, CHUNK, TILE, TILE))
    first = lax.all_to_all(four, AXES, 0, 0, tiled=True, axis_index_groups=first_groups())
    right = move(first, ring_pairs(-1))
    left = move(first, ring_pairs(1))
    far_a = move(right[:2], ring_pairs(-1))
    far_b = move(left[2:], ring_pairs(1))
    pieces = [first, right, far_a, far_b, left]
    pieces += [move(p, swap_pairs()) for p in pieces]
    packed = solve(pattern, pieces, blobs.reshape(NZ * NC, BLOCKS, 2, 2, 32, TILE))
    home_again = lax.all_to_all(packed, "col", 0, 0, tiled=True, axis_index_groups=groups)
    return finish(home_again, rhs_ext)


def solution(mesh):
    return jax.shard_map(
        local,
        mesh=mesh,
        in_specs=(
            P(None, "row", None),
            P("col", None),
            P("row", "col"),
            P(None, "row"),
            P(("row", "col"), None),
        ),
        out_specs=(P("col", None), P(("row", "col"), None)),
        check_vma=False,
    )
```

```python
import jax
import jax.numpy as jnp
from jax import lax
from jax.experimental import pallas as pl
from jax.experimental.pallas import tpu as pltpu
from jax.sharding import PartitionSpec as P

AXES = ("row", "col")
NX, NY, NZ, NC = 4, 4, 16, 2
TILE = 128
SUPER = 8
TPS = 4
NZ_DEV = 6
OWN = 2
RHS = 512
RZ = RHS // NZ
CHUNK = 15
EARLY = 11
RHS_AT = 10
INV0 = NZ_DEV * TILE
BLOB = INV0 + TPS * TILE
BLOCKS = NZ_DEV + TPS
F32 = jnp.float32
BF = jnp.bfloat16
VMEM = 60 * 1024 * 1024


def dev(y, x, z, k):
    return ((y % NY) * NX + x % NX) * (NZ * NC) + (z % NZ) * NC + k % NC


def every():
    for y in range(NY):
        for x in range(NX):
            for z in range(NZ):
                for k in range(NC):
                    yield y, x, z, k


def home(slot, y, z):
    if slot == 0:
        if y == 1:
            return 2, 8 + z
        return 3 - y, 4 + z
    if z < 4:
        return y, z
    if z < 8:
        return y, 7 + z
    if y == 1:
        return y, z
    return y, z - 4


def stride_groups():
    return [
        [dev(y, x, m + 4 * q, k) for y in pair for q in range(4)]
        for x in range(NX)
        for k in range(NC)
        for pair in ((0, 3), (1, 2))
        for m in range(4)
    ]


def near_groups():
    return [
        [dev(y, x, 4 * q + m, k) for m in range(4)]
        for y in range(NY)
        for x in range(NX)
        for k in range(NC)
        for q in range(4)
    ]


def first_groups():
    groups = []
    for z in range(NZ):
        for k in range(NC):
            for a in range(4):
                groups.append([dev(a, b, z, k) if k == 0 else dev(b, a, z, k) for b in range(4)])
    return groups


def ring_pairs(step):
    return [
        (dev(y, x, z, k), dev(y + step, x, z, k) if k == 0 else dev(y, x + step, z, k))
        for y, x, z, k in every()
    ]


def swap_pairs():
    return [(dev(y, x, z, k), dev(y, x, z, 1 - k)) for y, x, z, k in every()]


def move(value, pairs):
    return lax.ppermute(value, AXES, pairs)


def exchange(value, groups):
    return lax.all_to_all(value, AXES, 0, 0, tiled=True, axis_index_groups=groups)


def nt(a, b):
    return lax.dot_general(a, b, (((1,), (1,)), ((), ())), preferred_element_type=F32)


def coordinates():
    row, col = lax.axis_index("row"), lax.axis_index("col")
    return row >> 2, row & 3, col >> 1, col & 1


def prep_kernel(pattern, off, inv, rhs, blob, send, btile, flat):
    y, _, z, _ = coordinates()
    blob[:INV0] = off[...]
    for j in range(TPS):
        blob[INV0 + j * TILE : INV0 + (j + 1) * TILE] = inv[:, j * TILE : (j + 1) * TILE]
    tiles = []
    for slot in range(OWN):
        tile = jnp.zeros((TILE, TILE), F32)
        for k in range(NZ_DEV):
            block = off[k * TILE : (k + 1) * TILE].astype(F32)
            tile = jnp.where(pattern[z >> 1, k] == slot, block, tile)
        tiles.append(tile)
    for half in range(2):
        tile = jnp.where((y >> 1) == half, tiles[1], tiles[0]).astype(BF)
        for q in range(4):
            send[half * 4 + q] = tile
    start = pl.multiple_of(z * RZ, RZ)
    for slot in range(OWN):
        flat[...] = rhs[slot].T
        part = flat[pl.ds(start, RZ), :]
        high = part.astype(BF)
        btile[slot * 2 * RZ : slot * 2 * RZ + RZ] = high
        btile[slot * 2 * RZ + RZ : (slot + 1) * 2 * RZ] = (part - high.astype(F32)).astype(BF)


def prep(pattern, off, inv, rhs):
    tile = jax.ShapeDtypeStruct((TILE, TILE), BF)
    vm = pl.BlockSpec(memory_space=pltpu.VMEM)
    return pl.pallas_call(
        prep_kernel,
        out_shape=(
            jax.ShapeDtypeStruct((BLOB, TILE), BF),
            jax.ShapeDtypeStruct((8, TILE, TILE), BF),
            tile,
        ),
        in_specs=[pl.BlockSpec(memory_space=pltpu.SMEM), vm, vm, vm],
        out_specs=(vm, vm, vm),
        scratch_shapes=[pltpu.VMEM((RHS, TILE), F32)],
        compiler_params=pltpu.CompilerParams(vmem_limit_bytes=VMEM),
    )(pattern, off, inv, rhs)


PIECES = ((0, 4), (4, 4), (8, 2), (10, 2), (12, 4))


def solve_kernel(pattern, *refs):
    pieces = refs[:10]
    blobs, out, factor, invs, rows_ext, upd, ext, sol, early, late, isems, esems = refs[10:]
    my_y, my_x, _, core = coordinates()

    def load(first, count, sems):
        return [
            pltpu.make_async_copy(
                pieces[h * 5 + p].at[:, pl.ds(first, count)],
                factor.at[h, pl.ds(at, blocks), pl.ds(first, count)],
                sems.at[h * 5 + p],
            )
            for h in range(2)
            for p, (at, blocks) in enumerate(PIECES)
        ]

    first_loads = load(0, EARLY, early)
    last_loads = load(EARLY, CHUNK - EARLY, late)
    inv_loads, ext_loads = [], []
    for s in range(SUPER):
        four = pl.ds(s * TPS, TPS)
        inv_loads.append(
            pltpu.make_async_copy(
                blobs.at[four, pl.ds(NZ_DEV, TPS)], invs.at[four], isems.at[s]
            )
        )
        ext_loads.append(
            pltpu.make_async_copy(
                blobs.at[four, pl.ds(0, NZ_DEV), :, core], rows_ext.at[four], esems.at[s]
            )
        )
    for c in first_loads[:5] + inv_loads[:1] + first_loads[5:] + inv_loads[1:2] + last_loads:
        c.start()
    for c in inv_loads[2:] + ext_loads:
        c.start()
    upd[...] = jnp.zeros_like(upd)
    ext[...] = jnp.zeros_like(ext)
    for c in first_loads:
        c.wait()

    def position(parity, y, x):
        if parity == 0:
            return ((y - my_y) & 3) * 4 + x
        return ((x - my_x) & 3) * 4 + y

    def block(parity, y, x, place):
        return factor[parity ^ core, position(parity, y, x), place]

    def rhs_tile(t):
        slot, y, x = t // 16, t % 16 // NX, t % NX
        where = jnp.where(core == 0, position(0, y, x), position(1, y, x))
        base = slot * 2 * RZ
        high = factor[0, where, RHS_AT, base : base + RZ].astype(F32)
        low = factor[0, where, RHS_AT, base + RZ : base + 2 * RZ].astype(F32)
        return high + low

    for s in range(SUPER):
        inv_loads[s].wait()
        if s == 2:
            for c in last_loads:
                c.wait()
        current = jnp.concatenate(
            [(rhs_tile(t) - upd[t]).astype(BF) for t in range(s * TPS, (s + 1) * TPS)], axis=1
        )
        solved = []
        for i in range(TPS):
            c = s * TPS + i
            rows = jnp.concatenate(
                [invs[c, j].reshape(TILE, TILE) for j in range(i + 1)], axis=1
            )
            x_i = nt(current[:, : (i + 1) * TILE], rows).astype(BF)
            sol[c] = x_i
            solved.append(x_i)
        x_s = jnp.concatenate(solved, axis=1)
        for t in range((s + 1) * TPS, SUPER * TPS):
            slot, y, x = t // 16, t % 16 // NX, t % NX
            parts = []
            for j in range(TPS):
                at_y, place = home(slot, y, 2 * s + j // 2)
                parts.append(block(j % 2, at_y, x, place))
            upd[t] += nt(x_s, jnp.concatenate(parts, axis=1))
    for s in range(SUPER):
        ext_loads[s].wait()
        x_s = jnp.concatenate([sol[s * TPS + j] for j in range(TPS)], axis=1)
        for k in range(NZ_DEV):
            rows = jnp.concatenate(
                [rows_ext[s * TPS + j, k].reshape(64, TILE) for j in range(TPS)], axis=1
            )
            ext[pattern[s, k]] += nt(x_s, rows)
    for z in range(NZ):
        out[z, :RZ] = sol[2 * z + core]
        part = ext[OWN + z // 2][:, (z % 2) * 32 : (z % 2) * 32 + 32]
        high = part.astype(BF)
        low = (part - high.astype(F32)).astype(BF)
        both = jnp.concatenate([high, low], axis=1)
        out[z, RZ:] = jnp.concatenate([both[: RZ // 2], both[RZ // 2 :]], axis=1)


def solve(pattern, pieces, blobs):
    hbm = pl.BlockSpec(memory_space=pl.ANY)
    return pl.pallas_call(
        solve_kernel,
        out_shape=jax.ShapeDtypeStruct((NZ, RZ + RZ // 2, TILE), BF),
        in_specs=[pl.BlockSpec(memory_space=pltpu.SMEM)] + [hbm] * 11,
        out_specs=pl.BlockSpec(memory_space=pltpu.VMEM),
        scratch_shapes=[
            pltpu.VMEM((2, 16, CHUNK, TILE, TILE), BF),
            pltpu.VMEM((SUPER * TPS, TPS, 2, 2, 32, TILE), BF),
            pltpu.VMEM((SUPER * TPS, NZ_DEV, 2, 32, TILE), BF),
            pltpu.VMEM((SUPER * TPS, RZ, TILE), F32),
            pltpu.VMEM((10, RZ, 64), F32),
            pltpu.VMEM((SUPER * TPS, RZ, TILE), BF),
            pltpu.SemaphoreType.DMA((10,)),
            pltpu.SemaphoreType.DMA((10,)),
            pltpu.SemaphoreType.DMA((SUPER,)),
            pltpu.SemaphoreType.DMA((SUPER,)),
        ],
        compiler_params=pltpu.CompilerParams(vmem_limit_bytes=VMEM),
    )(pattern, *pieces, blobs)


def finish_kernel(got, rhs_ext, solution, remainder):
    x = jnp.concatenate([got[z, :RZ].astype(F32) for z in range(NZ)], axis=0)
    solution[...] = x.T.astype(BF)
    parts = []
    for z in range(NZ):
        both = got[z, RZ:].astype(F32)
        parts.append(both[:, :32] + both[:, 32:64])
        parts.append(both[:, 64:96] + both[:, 96:])
    remainder[...] = rhs_ext[...] - jnp.concatenate(parts, axis=0).T


def finish(got, rhs_ext):
    return pl.pallas_call(
        finish_kernel,
        out_shape=(
            jax.ShapeDtypeStruct((TILE, RHS), BF),
            jax.ShapeDtypeStruct((32, RHS), F32),
        ),
        compiler_params=pltpu.CompilerParams(vmem_limit_bytes=VMEM),
    )(got, rhs_ext)


def local(rhs_own, inverse, offdiag, pattern, rhs_ext):
    y, _, _, _ = coordinates()
    groups = [[NC * i + k for i in range(NZ)] for k in range(NC)]
    blob, send, btile = prep(pattern, offdiag, inverse, rhs_own)
    blobs = lax.all_gather(blob, "col")
    got = exchange(send, stride_groups())
    low = y < 2
    last = jnp.where(low, jnp.where(y == 0, got[5], got[2]), jnp.where(y == 2, got[0], got[7]))
    quad = jnp.stack(
        [
            jnp.where(low, got[0], got[4]),
            jnp.where(low, got[1], got[5]),
            jnp.where(low, got[4], got[6]),
            last,
        ]
    )
    line = exchange(jnp.broadcast_to(quad[None], (4, 4, TILE, TILE)), near_groups())
    chunk = jnp.concatenate(
        [line[:, 0], line[:, 2], line[:2, 3], btile[None], line[:, 1]], axis=0
    )
    four = jnp.broadcast_to(chunk[None], (4, CHUNK, TILE, TILE))
    first = exchange(four, first_groups())
    right = move(first, ring_pairs(-1))
    left = move(first, ring_pairs(1))
    far_a = move(right[:2], ring_pairs(-1))
    far_b = move(left[2:], ring_pairs(1))
    pieces = [first, right, far_a, far_b, left]
    pieces += [move(p, swap_pairs()) for p in pieces]
    packed = solve(pattern, pieces, blobs.reshape(NZ * NC, BLOCKS, 2, 2, 32, TILE))
    home_again = lax.all_to_all(packed, "col", 0, 0, tiled=True, axis_index_groups=groups)
    return finish(home_again, rhs_ext)


def solution(mesh):
    return jax.shard_map(
        local,
        mesh=mesh,
        in_specs=(
            P(None, "row", None),
            P("col", None),
            P("row", "col"),
            P(None, "row"),
            P(("row", "col"), None),
        ),
        out_specs=(P("col", None), P(("row", "col"), None)),
        check_vma=False,
    )
```

```python
import jax
import jax.numpy as jnp
from jax import lax
from jax.experimental import pallas as pl
from jax.experimental.pallas import tpu as pltpu
from jax.sharding import PartitionSpec as P

AXES = ("row", "col")
NX, NY, NZ, NC = 4, 4, 16, 2
TILE = 128
SUPER = 8
TPS = 4
NZ_DEV = 6
OWN = 2
RHS = 512
RZ = RHS // NZ
CHUNK = 15
EARLY = 11
RHS_AT = 10
INV0 = NZ_DEV * TILE
BLOB = INV0 + TPS * TILE
BLOCKS = NZ_DEV + TPS
F32 = jnp.float32
BF = jnp.bfloat16
VMEM = 60 * 1024 * 1024


def dev(y, x, z, k):
    return ((y % NY) * NX + x % NX) * (NZ * NC) + (z % NZ) * NC + k % NC


def every():
    for y in range(NY):
        for x in range(NX):
            for z in range(NZ):
                for k in range(NC):
                    yield y, x, z, k


def home(slot, y, z):
    if slot == 0:
        if y == 1:
            return 2, 8 + z
        return 3 - y, 4 + z
    if z < 4:
        return y, z
    if z < 8:
        return y, 7 + z
    if y == 1:
        return y, z
    return y, z - 4


def stride_groups():
    return [
        [dev(y, x, m + 4 * q, k) for y in pair for q in range(4)]
        for x in range(NX)
        for k in range(NC)
        for pair in ((0, 3), (1, 2))
        for m in range(4)
    ]


def near_groups():
    return [
        [dev(y, x, 4 * q + m, k) for m in range(4)]
        for y in range(NY)
        for x in range(NX)
        for k in range(NC)
        for q in range(4)
    ]


def first_groups():
    groups = []
    for z in range(NZ):
        for k in range(NC):
            for a in range(4):
                groups.append([dev(a, b, z, k) if k == 0 else dev(b, a, z, k) for b in range(4)])
    return groups


def ring_pairs(step):
    return [
        (dev(y, x, z, k), dev(y + step, x, z, k) if k == 0 else dev(y, x + step, z, k))
        for y, x, z, k in every()
    ]


def swap_pairs():
    return [(dev(y, x, z, k), dev(y, x, z, 1 - k)) for y, x, z, k in every()]


def move(value, pairs):
    return lax.ppermute(value, AXES, pairs)


def exchange(value, groups):
    return lax.all_to_all(value, AXES, 0, 0, tiled=True, axis_index_groups=groups)


def nt(a, b):
    return lax.dot_general(a, b, (((1,), (1,)), ((), ())), preferred_element_type=F32)


def coordinates():
    row, col = lax.axis_index("row"), lax.axis_index("col")
    return row >> 2, row & 3, col >> 1, col & 1


def prep_kernel(pattern, off, inv, rhs, blob, send, btile, flat):
    y, _, z, _ = coordinates()
    blob[:INV0] = off[...]
    for j in range(TPS):
        blob[INV0 + j * TILE : INV0 + (j + 1) * TILE] = inv[:, j * TILE : (j + 1) * TILE]
    tiles = []
    for slot in range(OWN):
        tile = jnp.zeros((TILE, TILE), F32)
        for k in range(NZ_DEV):
            block = off[k * TILE : (k + 1) * TILE].astype(F32)
            tile = jnp.where(pattern[z >> 1, k] == slot, block, tile)
        tiles.append(tile)
    for half in range(2):
        tile = jnp.where((y >> 1) == half, tiles[1], tiles[0]).astype(BF)
        for q in range(4):
            send[half * 4 + q] = tile
    start = pl.multiple_of(z * RZ, RZ)
    for slot in range(OWN):
        flat[...] = rhs[slot].T
        part = flat[pl.ds(start, RZ), :]
        high = part.astype(BF)
        btile[slot * 2 * RZ : slot * 2 * RZ + RZ] = high
        btile[slot * 2 * RZ + RZ : (slot + 1) * 2 * RZ] = (part - high.astype(F32)).astype(BF)


def prep(pattern, off, inv, rhs):
    tile = jax.ShapeDtypeStruct((TILE, TILE), BF)
    vm = pl.BlockSpec(memory_space=pltpu.VMEM)
    return pl.pallas_call(
        prep_kernel,
        out_shape=(
            jax.ShapeDtypeStruct((BLOB, TILE), BF),
            jax.ShapeDtypeStruct((8, TILE, TILE), BF),
            tile,
        ),
        in_specs=[pl.BlockSpec(memory_space=pltpu.SMEM), vm, vm, vm],
        out_specs=(vm, vm, vm),
        scratch_shapes=[pltpu.VMEM((RHS, TILE), F32)],
        compiler_params=pltpu.CompilerParams(vmem_limit_bytes=VMEM),
    )(pattern, off, inv, rhs)


PIECES = ((0, 4), (4, 4), (8, 2), (10, 2), (12, 4))


def solve_kernel(pattern, *refs):
    pieces = refs[:10]
    blobs, out, factor, invs, rows_ext, upd, ext, sol, early, late, isems, esems = refs[10:]
    my_y, my_x, _, core = coordinates()

    def load(first, count, sems):
        return [
            pltpu.make_async_copy(
                pieces[h * 5 + p].at[:, pl.ds(first, count)],
                factor.at[h, pl.ds(at, blocks), pl.ds(first, count)],
                sems.at[h * 5 + p],
            )
            for h in range(2)
            for p, (at, blocks) in enumerate(PIECES)
        ]

    first_loads = load(0, EARLY, early)
    last_loads = load(EARLY, CHUNK - EARLY, late)
    inv_loads, ext_loads = [], []
    for s in range(SUPER):
        four = pl.ds(s * TPS, TPS)
        inv_loads.append(
            pltpu.make_async_copy(
                blobs.at[four, pl.ds(NZ_DEV, TPS)], invs.at[four], isems.at[s]
            )
        )
        ext_loads.append(
            pltpu.make_async_copy(
                blobs.at[four, pl.ds(0, NZ_DEV), :, core], rows_ext.at[four], esems.at[s]
            )
        )
    for c in first_loads[:5] + inv_loads[:1] + first_loads[5:] + inv_loads[1:2] + last_loads:
        c.start()
    for c in inv_loads[2:] + ext_loads:
        c.start()
    upd[...] = jnp.zeros_like(upd)
    ext[...] = jnp.zeros_like(ext)
    for c in first_loads:
        c.wait()

    def position(parity, y, x):
        if parity == 0:
            return ((y - my_y) & 3) * 4 + x
        return ((x - my_x) & 3) * 4 + y

    def block(parity, y, x, place):
        return factor[parity ^ core, position(parity, y, x), place]

    def rhs_tile(t):
        slot, y, x = t // 16, t % 16 // NX, t % NX
        where = jnp.where(core == 0, position(0, y, x), position(1, y, x))
        base = slot * 2 * RZ
        high = factor[0, where, RHS_AT, base : base + RZ].astype(F32)
        low = factor[0, where, RHS_AT, base + RZ : base + 2 * RZ].astype(F32)
        return high + low

    for s in range(SUPER):
        inv_loads[s].wait()
        if s == 2:
            for c in last_loads:
                c.wait()
        current = jnp.concatenate(
            [(rhs_tile(t) - upd[t]).astype(BF) for t in range(s * TPS, (s + 1) * TPS)], axis=1
        )
        solved = []
        for i in range(TPS):
            c = s * TPS + i
            rows = jnp.concatenate(
                [invs[c, j].reshape(TILE, TILE) for j in range(i + 1)], axis=1
            )
            x_i = nt(current[:, : (i + 1) * TILE], rows).astype(BF)
            sol[c] = x_i
            solved.append(x_i)
        x_s = jnp.concatenate(solved, axis=1)
        for t in range((s + 1) * TPS, SUPER * TPS):
            slot, y, x = t // 16, t % 16 // NX, t % NX
            parts = []
            for j in range(TPS):
                at_y, place = home(slot, y, 2 * s + j // 2)
                parts.append(block(j % 2, at_y, x, place))
            upd[t] += nt(x_s, jnp.concatenate(parts, axis=1))
    for s in range(SUPER):
        ext_loads[s].wait()
        x_s = jnp.concatenate([sol[s * TPS + j] for j in range(TPS)], axis=1)
        for k in range(NZ_DEV):
            rows = jnp.concatenate(
                [rows_ext[s * TPS + j, k].reshape(64, TILE) for j in range(TPS)], axis=1
            )
            ext[pattern[s, k]] += nt(x_s, rows)
    for z in range(NZ):
        out[z, :RZ] = sol[2 * z + core]
        part = ext[OWN + z // 2][:, (z % 2) * 32 : (z % 2) * 32 + 32]
        high = part.astype(BF)
        low = (part - high.astype(F32)).astype(BF)
        both = jnp.concatenate([high, low], axis=1)
        out[z, RZ:] = jnp.concatenate([both[: RZ // 2], both[RZ // 2 :]], axis=1)


def solve(pattern, pieces, blobs):
    hbm = pl.BlockSpec(memory_space=pl.ANY)
    return pl.pallas_call(
        solve_kernel,
        out_shape=jax.ShapeDtypeStruct((NZ, RZ + RZ // 2, TILE), BF),
        in_specs=[pl.BlockSpec(memory_space=pltpu.SMEM)] + [hbm] * 11,
        out_specs=pl.BlockSpec(memory_space=pltpu.VMEM),
        scratch_shapes=[
            pltpu.VMEM((2, 16, CHUNK, TILE, TILE), BF),
            pltpu.VMEM((SUPER * TPS, TPS, 2, 2, 32, TILE), BF),
            pltpu.VMEM((SUPER * TPS, NZ_DEV, 2, 32, TILE), BF),
            pltpu.VMEM((SUPER * TPS, RZ, TILE), F32),
            pltpu.VMEM((10, RZ, 64), F32),
            pltpu.VMEM((SUPER * TPS, RZ, TILE), BF),
            pltpu.SemaphoreType.DMA((10,)),
            pltpu.SemaphoreType.DMA((10,)),
            pltpu.SemaphoreType.DMA((SUPER,)),
            pltpu.SemaphoreType.DMA((SUPER,)),
        ],
        compiler_params=pltpu.CompilerParams(vmem_limit_bytes=VMEM),
    )(pattern, *pieces, blobs)


def finish_kernel(got, rhs_ext, solution, remainder):
    x = jnp.concatenate([got[z, :RZ].astype(F32) for z in range(NZ)], axis=0)
    solution[...] = x.T.astype(BF)
    parts = []
    for z in range(NZ):
        both = got[z, RZ:].astype(F32)
        parts.append(both[:, :32] + both[:, 32:64])
        parts.append(both[:, 64:96] + both[:, 96:])
    remainder[...] = rhs_ext[...] - jnp.concatenate(parts, axis=0).T


def finish(got, rhs_ext):
    return pl.pallas_call(
        finish_kernel,
        out_shape=(
            jax.ShapeDtypeStruct((TILE, RHS), BF),
            jax.ShapeDtypeStruct((32, RHS), F32),
        ),
        compiler_params=pltpu.CompilerParams(vmem_limit_bytes=VMEM),
    )(got, rhs_ext)


def local(rhs_own, inverse, offdiag, pattern, rhs_ext):
    y, _, _, _ = coordinates()
    groups = [[NC * i + k for i in range(NZ)] for k in range(NC)]
    blob, send, btile = prep(pattern, offdiag, inverse, rhs_own)
    got = exchange(send, stride_groups())
    low = y < 2
    last = jnp.where(low, jnp.where(y == 0, got[5], got[2]), jnp.where(y == 2, got[0], got[7]))
    quad = jnp.stack(
        [
            jnp.where(low, got[0], got[4]),
            jnp.where(low, got[1], got[5]),
            jnp.where(low, got[4], got[6]),
            last,
        ]
    )
    line = exchange(jnp.broadcast_to(quad[None], (4, 4, TILE, TILE)), near_groups())
    blob, line = lax.optimization_barrier((blob, line))
    blobs = lax.all_gather(blob, "col")
    chunk = jnp.concatenate(
        [line[:, 0], line[:, 2], line[:2, 3], btile[None], line[:, 1]], axis=0
    )
    four = jnp.broadcast_to(chunk[None], (4, CHUNK, TILE, TILE))
    first = exchange(four, first_groups())
    right = move(first, ring_pairs(-1))
    left = move(first, ring_pairs(1))
    far_a = move(right[:2], ring_pairs(-1))
    far_b = move(left[2:], ring_pairs(1))
    pieces = [first, right, far_a, far_b, left]
    pieces += [move(p, swap_pairs()) for p in pieces]
    packed = solve(pattern, pieces, blobs.reshape(NZ * NC, BLOCKS, 2, 2, 32, TILE))
    home_again = lax.all_to_all(packed, "col", 0, 0, tiled=True, axis_index_groups=groups)
    return finish(home_again, rhs_ext)


def solution(mesh):
    return jax.shard_map(
        local,
        mesh=mesh,
        in_specs=(
            P(None, "row", None),
            P("col", None),
            P("row", "col"),
            P(None, "row"),
            P(("row", "col"), None),
        ),
        out_specs=(P("col", None), P(("row", "col"), None)),
        check_vma=False,
    )
```

```python
import jax
import jax.numpy as jnp
from jax import lax
from jax.experimental import pallas as pl
from jax.experimental.pallas import tpu as pltpu
from jax.sharding import PartitionSpec as P

AXES = ("row", "col")
NX, NY, NZ, NC = 4, 4, 16, 2
TILE = 128
SUPER = 8
TPS = 4
NZ_DEV = 6
OWN = 2
RHS = 512
RZ = RHS // NZ
CHUNK = 15
RHS_AT = 6
WAVES = ((0, 7), (7, 4), (11, 4))
INV0 = NZ_DEV * TILE
BLOB = INV0 + TPS * TILE
BLOCKS = NZ_DEV + TPS
F32 = jnp.float32
BF = jnp.bfloat16
VMEM = 60 * 1024 * 1024


def dev(y, x, z, k):
    return ((y % NY) * NX + x % NX) * (NZ * NC) + (z % NZ) * NC + k % NC


def every():
    for y in range(NY):
        for x in range(NX):
            for z in range(NZ):
                for k in range(NC):
                    yield y, x, z, k


def home(slot, y, z):
    first, second, third, fourth = (0, 1, 7, 8), (11, 12, 13, 14), (2, 3, 9, 10), (4, 5)
    if slot == 0:
        if y == 1:
            return 2, fourth[z]
        return 3 - y, (third + fourth)[z]
    if z < 8:
        return y, (first + second)[z]
    if y == 1:
        return y, fourth[z - 8]
    return y, (third + fourth)[z - 8]


def stride_groups():
    return [
        [dev(y, x, m + 4 * q, k) for y in pair for q in range(4)]
        for x in range(NX)
        for k in range(NC)
        for pair in ((0, 3), (1, 2))
        for m in range(4)
    ]


def near_groups():
    return [
        [dev(y, x, 4 * q + m, k) for m in range(4)]
        for y in range(NY)
        for x in range(NX)
        for k in range(NC)
        for q in range(4)
    ]


def first_groups():
    groups = []
    for z in range(NZ):
        for k in range(NC):
            for a in range(4):
                groups.append([dev(a, b, z, k) if k == 0 else dev(b, a, z, k) for b in range(4)])
    return groups


def ring_pairs(step):
    return [
        (dev(y, x, z, k), dev(y + step, x, z, k) if k == 0 else dev(y, x + step, z, k))
        for y, x, z, k in every()
    ]


def swap_pairs():
    return [(dev(y, x, z, k), dev(y, x, z, 1 - k)) for y, x, z, k in every()]


def move(value, pairs):
    return lax.ppermute(value, AXES, pairs)


def exchange(value, groups):
    return lax.all_to_all(value, AXES, 0, 0, tiled=True, axis_index_groups=groups)


def nt(a, b):
    return lax.dot_general(a, b, (((1,), (1,)), ((), ())), preferred_element_type=F32)


def coordinates():
    row, col = lax.axis_index("row"), lax.axis_index("col")
    return row >> 2, row & 3, col >> 1, col & 1


def pick_kernel(pattern, off, send):
    y, _, z, _ = coordinates()
    tiles = []
    for slot in range(OWN):
        tile = jnp.zeros((TILE, TILE), F32)
        for k in range(NZ_DEV):
            block = off[k * TILE : (k + 1) * TILE].astype(F32)
            tile = jnp.where(pattern[z >> 1, k] == slot, block, tile)
        tiles.append(tile)
    for half in range(2):
        tile = jnp.where((y >> 1) == half, tiles[1], tiles[0]).astype(BF)
        for q in range(4):
            send[half * 4 + q] = tile


def pick(pattern, off):
    vm = pl.BlockSpec(memory_space=pltpu.VMEM)
    return pl.pallas_call(
        pick_kernel,
        out_shape=jax.ShapeDtypeStruct((8, TILE, TILE), BF),
        in_specs=[pl.BlockSpec(memory_space=pltpu.SMEM), vm],
        out_specs=vm,
        compiler_params=pltpu.CompilerParams(vmem_limit_bytes=VMEM),
    )(pattern, off)


def prep_kernel(off, inv, rhs, blob, btile, flat):
    _, _, z, _ = coordinates()
    blob[:INV0] = off[...]
    for j in range(TPS):
        blob[INV0 + j * TILE : INV0 + (j + 1) * TILE] = inv[:, j * TILE : (j + 1) * TILE]
    start = pl.multiple_of(z * RZ, RZ)
    for slot in range(OWN):
        flat[...] = rhs[slot].T
        part = flat[pl.ds(start, RZ), :]
        high = part.astype(BF)
        btile[slot * 2 * RZ : slot * 2 * RZ + RZ] = high
        btile[slot * 2 * RZ + RZ : (slot + 1) * 2 * RZ] = (part - high.astype(F32)).astype(BF)


def prep(off, inv, rhs):
    vm = pl.BlockSpec(memory_space=pltpu.VMEM)
    return pl.pallas_call(
        prep_kernel,
        out_shape=(
            jax.ShapeDtypeStruct((BLOB, TILE), BF),
            jax.ShapeDtypeStruct((TILE, TILE), BF),
        ),
        in_specs=[vm, vm, vm],
        out_specs=(vm, vm),
        scratch_shapes=[pltpu.VMEM((RHS, TILE), F32)],
        compiler_params=pltpu.CompilerParams(vmem_limit_bytes=VMEM),
        cost_estimate=pl.CostEstimate(flops=1 << 20, bytes_accessed=4 << 20, transcendentals=0),
    )(off, inv, rhs)


PIECES = ((0, 4), (4, 4), (8, 2), (10, 2), (12, 4))


def solve_kernel(pattern, *refs):
    pieces = refs[:10]
    blobs, out, factor, invs, rows_ext, upd, ext, sol, *wsems, isems, esems = refs[10:]
    my_y, my_x, _, core = coordinates()

    def load(first, count, sems):
        return [
            pltpu.make_async_copy(
                pieces[h * 5 + p].at[:, pl.ds(first, count)],
                factor.at[h, pl.ds(at, blocks), pl.ds(first, count)],
                sems.at[h * 5 + p],
            )
            for h in range(2)
            for p, (at, blocks) in enumerate(PIECES)
        ]

    waves = [load(first, count, sems) for (first, count), sems in zip(WAVES, wsems)]
    inv_loads, ext_loads = [], []
    for s in range(SUPER):
        four = pl.ds(s * TPS, TPS)
        inv_loads.append(
            pltpu.make_async_copy(
                blobs.at[four, pl.ds(NZ_DEV, TPS)], invs.at[four], isems.at[s]
            )
        )
        ext_loads.append(
            pltpu.make_async_copy(
                blobs.at[four, pl.ds(0, NZ_DEV), :, core], rows_ext.at[four], esems.at[s]
            )
        )
    for wave, inv_load in zip(waves, inv_loads):
        for c in wave + [inv_load]:
            c.start()
    for c in inv_loads[len(WAVES) :] + ext_loads:
        c.start()
    upd[...] = jnp.zeros_like(upd)
    ext[...] = jnp.zeros_like(ext)
    def position(parity, y, x):
        if parity == 0:
            return ((y - my_y) & 3) * 4 + x
        return ((x - my_x) & 3) * 4 + y

    def block(parity, y, x, place):
        return factor[parity ^ core, position(parity, y, x), place]

    def rhs_tile(t):
        slot, y, x = t // 16, t % 16 // NX, t % NX
        where = jnp.where(core == 0, position(0, y, x), position(1, y, x))
        base = slot * 2 * RZ
        high = factor[0, where, RHS_AT, base : base + RZ].astype(F32)
        low = factor[0, where, RHS_AT, base + RZ : base + 2 * RZ].astype(F32)
        return high + low

    for s in range(SUPER):
        if s < len(WAVES):
            for c in waves[s]:
                c.wait()
        inv_loads[s].wait()
        current = jnp.concatenate(
            [(rhs_tile(t) - upd[t]).astype(BF) for t in range(s * TPS, (s + 1) * TPS)], axis=1
        )
        solved = []
        for i in range(TPS):
            c = s * TPS + i
            rows = jnp.concatenate(
                [invs[c, j].reshape(TILE, TILE) for j in range(i + 1)], axis=1
            )
            x_i = nt(current[:, : (i + 1) * TILE], rows).astype(BF)
            sol[c] = x_i
            solved.append(x_i)
        x_s = jnp.concatenate(solved, axis=1)
        for t in range((s + 1) * TPS, SUPER * TPS, 2):
            rows = []
            for n in range(2):
                slot, y, x = (t + n) // 16, (t + n) % 16 // NX, (t + n) % NX
                parts = []
                for j in range(TPS):
                    at_y, place = home(slot, y, 2 * s + j // 2)
                    parts.append(block(j % 2, at_y, x, place))
                rows.append(jnp.concatenate(parts, axis=1))
            more = nt(x_s, jnp.concatenate(rows, axis=0))
            for n in range(2):
                upd[t + n] += more[:, n * TILE : (n + 1) * TILE]
    for s in range(SUPER):
        ext_loads[s].wait()
        x_s = jnp.concatenate([sol[s * TPS + j] for j in range(TPS)], axis=1)
        for k in range(NZ_DEV):
            rows = jnp.concatenate(
                [rows_ext[s * TPS + j, k].reshape(64, TILE) for j in range(TPS)], axis=1
            )
            ext[pattern[s, k]] += nt(x_s, rows)
    for z in range(NZ):
        out[z, :RZ] = sol[2 * z + core]
        part = ext[OWN + z // 2][:, (z % 2) * 32 : (z % 2) * 32 + 32]
        high = part.astype(BF)
        low = (part - high.astype(F32)).astype(BF)
        both = jnp.concatenate([high, low], axis=1)
        out[z, RZ:] = jnp.concatenate([both[: RZ // 2], both[RZ // 2 :]], axis=1)


def solve(pattern, pieces, blobs):
    hbm = pl.BlockSpec(memory_space=pl.ANY)
    return pl.pallas_call(
        solve_kernel,
        out_shape=jax.ShapeDtypeStruct((NZ, RZ + RZ // 2, TILE), BF),
        in_specs=[pl.BlockSpec(memory_space=pltpu.SMEM)] + [hbm] * 11,
        out_specs=pl.BlockSpec(memory_space=pltpu.VMEM),
        scratch_shapes=[
            pltpu.VMEM((2, 16, CHUNK, TILE, TILE), BF),
            pltpu.VMEM((SUPER * TPS, TPS, 2, 2, 32, TILE), BF),
            pltpu.VMEM((SUPER * TPS, NZ_DEV, 2, 32, TILE), BF),
            pltpu.VMEM((SUPER * TPS, RZ, TILE), F32),
            pltpu.VMEM((10, RZ, 64), F32),
            pltpu.VMEM((SUPER * TPS, RZ, TILE), BF),
            pltpu.SemaphoreType.DMA((10,)),
            pltpu.SemaphoreType.DMA((10,)),
            pltpu.SemaphoreType.DMA((10,)),
            pltpu.SemaphoreType.DMA((SUPER,)),
            pltpu.SemaphoreType.DMA((SUPER,)),
        ],
        compiler_params=pltpu.CompilerParams(vmem_limit_bytes=VMEM),
    )(pattern, *pieces, blobs)


def finish_kernel(got, rhs_ext, solution, remainder):
    x = jnp.concatenate([got[z, :RZ].astype(F32) for z in range(NZ)], axis=0)
    solution[...] = x.T.astype(BF)
    parts = []
    for z in range(NZ):
        both = got[z, RZ:].astype(F32)
        parts.append(both[:, :32] + both[:, 32:64])
        parts.append(both[:, 64:96] + both[:, 96:])
    remainder[...] = rhs_ext[...] - jnp.concatenate(parts, axis=0).T


def finish(got, rhs_ext):
    return pl.pallas_call(
        finish_kernel,
        out_shape=(
            jax.ShapeDtypeStruct((TILE, RHS), BF),
            jax.ShapeDtypeStruct((32, RHS), F32),
        ),
        compiler_params=pltpu.CompilerParams(vmem_limit_bytes=VMEM),
    )(got, rhs_ext)


def local(rhs_own, inverse, offdiag, pattern, rhs_ext):
    y, _, _, _ = coordinates()
    groups = [[NC * i + k for i in range(NZ)] for k in range(NC)]
    got = exchange(pick(pattern, offdiag), stride_groups())
    blob, btile = prep(offdiag, inverse, rhs_own)
    low = y < 2
    last = jnp.where(low, jnp.where(y == 0, got[5], got[2]), jnp.where(y == 2, got[0], got[7]))
    quad = jnp.stack(
        [
            jnp.where(low, got[0], got[4]),
            jnp.where(low, got[1], got[5]),
            jnp.where(low, got[4], got[6]),
            last,
        ]
    )
    line = lax.all_gather(quad, AXES, axis_index_groups=near_groups())
    blob, line = lax.optimization_barrier((blob, line))
    blobs = lax.all_gather(blob, "col")
    chunk = jnp.concatenate(
        [
            line[:2, 0],
            line[:2, 2],
            line[:2, 3],
            btile[None],
            line[2:, 0],
            line[2:, 2],
            line[:, 1],
        ],
        axis=0,
    )
    four = jnp.broadcast_to(chunk[None], (4, CHUNK, TILE, TILE))
    first = exchange(four, first_groups())
    right = move(first, ring_pairs(-1))
    left = move(first, ring_pairs(1))
    far_a = move(right[:2], ring_pairs(-1))
    far_b = move(left[2:], ring_pairs(1))
    pieces = [first, right, far_a, far_b, left]
    pieces += [move(p, swap_pairs()) for p in pieces]
    packed = solve(pattern, pieces, blobs.reshape(NZ * NC, BLOCKS, 2, 2, 32, TILE))
    home_again = lax.all_to_all(packed, "col", 0, 0, tiled=True, axis_index_groups=groups)
    return finish(home_again, rhs_ext)


def solution(mesh):
    return jax.shard_map(
        local,
        mesh=mesh,
        in_specs=(
            P(None, "row", None),
            P("col", None),
            P("row", "col"),
            P(None, "row"),
            P(("row", "col"), None),
        ),
        out_specs=(P("col", None), P(("row", "col"), None)),
        check_vma=False,
    )
```

```python
import jax
import jax.numpy as jnp
from jax import lax
from jax.experimental import pallas as pl
from jax.experimental.pallas import tpu as pltpu
from jax.sharding import PartitionSpec as P

AXES = ("row", "col")
NX, NY, NZ, NC = 4, 4, 16, 2
TILE = 128
SUPER = 8
TPS = 4
NZ_DEV = 6
OWN = 2
RHS = 512
RZ = RHS // NZ
CHUNK = 15
RHS_AT = 6
WAVES = ((0, 7), (7, 4), (11, 4))
INV0 = NZ_DEV * TILE
BLOB = INV0 + TPS * TILE
BLOCKS = NZ_DEV + TPS
F32 = jnp.float32
BF = jnp.bfloat16
VMEM = 60 * 1024 * 1024


def dev(y, x, z, k):
    return ((y % NY) * NX + x % NX) * (NZ * NC) + (z % NZ) * NC + k % NC


def every():
    for y in range(NY):
        for x in range(NX):
            for z in range(NZ):
                for k in range(NC):
                    yield y, x, z, k


def home(slot, y, z):
    first, second, third, fourth = (0, 1, 7, 8), (11, 12, 13, 14), (2, 3, 9, 10), (4, 5)
    if slot == 0:
        if y == 1:
            return 2, fourth[z]
        return 3 - y, (third + fourth)[z]
    if z < 8:
        return y, (first + second)[z]
    if y == 1:
        return y, fourth[z - 8]
    return y, (third + fourth)[z - 8]


def stride_groups():
    return [
        [dev(y, x, m + 4 * q, k) for y in pair for q in range(4)]
        for x in range(NX)
        for k in range(NC)
        for pair in ((0, 3), (1, 2))
        for m in range(4)
    ]


def near_groups():
    return [
        [dev(y, x, 4 * q + m, k) for m in range(4)]
        for y in range(NY)
        for x in range(NX)
        for k in range(NC)
        for q in range(4)
    ]


def first_groups():
    groups = []
    for z in range(NZ):
        for k in range(NC):
            for a in range(4):
                groups.append([dev(a, b, z, k) if k == 0 else dev(b, a, z, k) for b in range(4)])
    return groups


def ring_pairs(step):
    return [
        (dev(y, x, z, k), dev(y + step, x, z, k) if k == 0 else dev(y, x + step, z, k))
        for y, x, z, k in every()
    ]


def swap_pairs():
    return [(dev(y, x, z, k), dev(y, x, z, 1 - k)) for y, x, z, k in every()]


def move(value, pairs):
    return lax.ppermute(value, AXES, pairs)


def exchange(value, groups):
    return lax.all_to_all(value, AXES, 0, 0, tiled=True, axis_index_groups=groups)


def nt(a, b):
    return lax.dot_general(a, b, (((1,), (1,)), ((), ())), preferred_element_type=F32)


def coordinates():
    row, col = lax.axis_index("row"), lax.axis_index("col")
    return row >> 2, row & 3, col >> 1, col & 1


def pick_kernel(pattern, off, send):
    y, _, z, _ = coordinates()
    tiles = []
    for slot in range(OWN):
        tile = jnp.zeros((TILE, TILE), F32)
        for k in range(NZ_DEV):
            block = off[k * TILE : (k + 1) * TILE].astype(F32)
            tile = jnp.where(pattern[z >> 1, k] == slot, block, tile)
        tiles.append(tile)
    for half in range(2):
        tile = jnp.where((y >> 1) == half, tiles[1], tiles[0]).astype(BF)
        for q in range(4):
            send[half * 4 + q] = tile


def pick(pattern, off):
    vm = pl.BlockSpec(memory_space=pltpu.VMEM)
    return pl.pallas_call(
        pick_kernel,
        out_shape=jax.ShapeDtypeStruct((8, TILE, TILE), BF),
        in_specs=[pl.BlockSpec(memory_space=pltpu.SMEM), vm],
        out_specs=vm,
        compiler_params=pltpu.CompilerParams(vmem_limit_bytes=VMEM),
    )(pattern, off)


def prep_kernel(off, inv, rhs, blob, btile, flat):
    _, _, z, _ = coordinates()
    blob[:INV0] = off[...]
    for j in range(TPS):
        blob[INV0 + j * TILE : INV0 + (j + 1) * TILE] = inv[:, j * TILE : (j + 1) * TILE]
    start = pl.multiple_of(z * RZ, RZ)
    for slot in range(OWN):
        flat[...] = rhs[slot].T
        part = flat[pl.ds(start, RZ), :]
        high = part.astype(BF)
        btile[slot * 2 * RZ : slot * 2 * RZ + RZ] = high
        btile[slot * 2 * RZ + RZ : (slot + 1) * 2 * RZ] = (part - high.astype(F32)).astype(BF)


def prep(off, inv, rhs):
    vm = pl.BlockSpec(memory_space=pltpu.VMEM)
    return pl.pallas_call(
        prep_kernel,
        out_shape=(
            jax.ShapeDtypeStruct((BLOB, TILE), BF),
            jax.ShapeDtypeStruct((TILE, TILE), BF),
        ),
        in_specs=[vm, vm, vm],
        out_specs=(vm, vm),
        scratch_shapes=[pltpu.VMEM((RHS, TILE), F32)],
        compiler_params=pltpu.CompilerParams(vmem_limit_bytes=VMEM),
        cost_estimate=pl.CostEstimate(flops=1 << 20, bytes_accessed=4 << 20, transcendentals=0),
    )(off, inv, rhs)


PIECES = ((0, 4), (4, 4), (8, 2), (10, 2), (12, 4))


def solve_kernel(pattern, *refs):
    pieces = refs[:10]
    blobs, out, factor, invs, rows_ext, upd, ext, sol, *wsems, isems, esems = refs[10:]
    my_y, my_x, _, core = coordinates()

    def load(first, count, sems):
        return [
            pltpu.make_async_copy(
                pieces[h * 5 + p].at[:, pl.ds(first, count)],
                factor.at[h, pl.ds(at, blocks), pl.ds(first, count)],
                sems.at[h * 5 + p],
            )
            for h in range(2)
            for p, (at, blocks) in enumerate(PIECES)
        ]

    waves = [load(first, count, sems) for (first, count), sems in zip(WAVES, wsems)]
    inv_loads, inv_lows, ext_loads = [], [], []
    for s in range(SUPER):
        four = pl.ds(s * TPS, TPS)
        inv_loads.append(
            pltpu.make_async_copy(
                blobs.at[four, pl.ds(NZ_DEV, 2)], invs.at[four, pl.ds(0, 2)], isems.at[2 * s]
            )
        )
        lower = pl.ds(s * TPS + 2, 2)
        inv_lows.append(
            pltpu.make_async_copy(
                blobs.at[lower, pl.ds(NZ_DEV + 2, 2)],
                invs.at[lower, pl.ds(2, 2)],
                isems.at[2 * s + 1],
            )
        )
        ext_loads.append(
            pltpu.make_async_copy(
                blobs.at[four, pl.ds(0, NZ_DEV), :, core], rows_ext.at[four], esems.at[s]
            )
        )
    for wave, inv_load, inv_low in zip(waves, inv_loads, inv_lows):
        for c in wave + [inv_load, inv_low]:
            c.start()
    for c in inv_loads[len(WAVES) :] + inv_lows[len(WAVES) :] + ext_loads:
        c.start()
    upd[...] = jnp.zeros_like(upd)
    ext[...] = jnp.zeros_like(ext)
    def position(parity, y, x):
        if parity == 0:
            return ((y - my_y) & 3) * 4 + x
        return ((x - my_x) & 3) * 4 + y

    def block(parity, y, x, place):
        return factor[parity ^ core, position(parity, y, x), place]

    def rhs_tile(t):
        slot, y, x = t // 16, t % 16 // NX, t % NX
        where = jnp.where(core == 0, position(0, y, x), position(1, y, x))
        base = slot * 2 * RZ
        high = factor[0, where, RHS_AT, base : base + RZ].astype(F32)
        low = factor[0, where, RHS_AT, base + RZ : base + 2 * RZ].astype(F32)
        return high + low

    for s in range(SUPER):
        if s < len(WAVES):
            for c in waves[s]:
                c.wait()
        inv_loads[s].wait()
        inv_lows[s].wait()
        current = jnp.concatenate(
            [(rhs_tile(t) - upd[t]).astype(BF) for t in range(s * TPS, (s + 1) * TPS)], axis=1
        )
        solved = []
        for i in range(TPS):
            c = s * TPS + i
            rows = jnp.concatenate(
                [invs[c, j].reshape(TILE, TILE) for j in range(i + 1)], axis=1
            )
            x_i = nt(current[:, : (i + 1) * TILE], rows).astype(BF)
            sol[c] = x_i
            solved.append(x_i)
        x_s = jnp.concatenate(solved, axis=1)
        for t in range((s + 1) * TPS, SUPER * TPS, 2):
            rows = []
            for n in range(2):
                slot, y, x = (t + n) // 16, (t + n) % 16 // NX, (t + n) % NX
                parts = []
                for j in range(TPS):
                    at_y, place = home(slot, y, 2 * s + j // 2)
                    parts.append(block(j % 2, at_y, x, place))
                rows.append(jnp.concatenate(parts, axis=1))
            more = nt(x_s, jnp.concatenate(rows, axis=0))
            for n in range(2):
                upd[t + n] += more[:, n * TILE : (n + 1) * TILE]
    for s in range(SUPER):
        ext_loads[s].wait()
        x_s = jnp.concatenate([sol[s * TPS + j] for j in range(TPS)], axis=1)
        for k in range(NZ_DEV):
            rows = jnp.concatenate(
                [rows_ext[s * TPS + j, k].reshape(64, TILE) for j in range(TPS)], axis=1
            )
            ext[pattern[s, k]] += nt(x_s, rows)
    for z in range(NZ):
        out[z, :RZ] = sol[2 * z + core]
        part = ext[OWN + z // 2][:, (z % 2) * 32 : (z % 2) * 32 + 32]
        high = part.astype(BF)
        low = (part - high.astype(F32)).astype(BF)
        both = jnp.concatenate([high, low], axis=1)
        out[z, RZ:] = jnp.concatenate([both[: RZ // 2], both[RZ // 2 :]], axis=1)


def solve(pattern, pieces, blobs):
    hbm = pl.BlockSpec(memory_space=pl.ANY)
    return pl.pallas_call(
        solve_kernel,
        out_shape=jax.ShapeDtypeStruct((NZ, RZ + RZ // 2, TILE), BF),
        in_specs=[pl.BlockSpec(memory_space=pltpu.SMEM)] + [hbm] * 11,
        out_specs=pl.BlockSpec(memory_space=pltpu.VMEM),
        scratch_shapes=[
            pltpu.VMEM((2, 16, CHUNK, TILE, TILE), BF),
            pltpu.VMEM((SUPER * TPS, TPS, 2, 2, 32, TILE), BF),
            pltpu.VMEM((SUPER * TPS, NZ_DEV, 2, 32, TILE), BF),
            pltpu.VMEM((SUPER * TPS, RZ, TILE), F32),
            pltpu.VMEM((10, RZ, 64), F32),
            pltpu.VMEM((SUPER * TPS, RZ, TILE), BF),
            pltpu.SemaphoreType.DMA((10,)),
            pltpu.SemaphoreType.DMA((10,)),
            pltpu.SemaphoreType.DMA((10,)),
            pltpu.SemaphoreType.DMA((2 * SUPER,)),
            pltpu.SemaphoreType.DMA((SUPER,)),
        ],
        compiler_params=pltpu.CompilerParams(vmem_limit_bytes=VMEM),
    )(pattern, *pieces, blobs)


def finish_kernel(got, rhs_ext, solution, remainder):
    x = jnp.concatenate([got[z, :RZ].astype(F32) for z in range(NZ)], axis=0)
    solution[...] = x.T.astype(BF)
    parts = []
    for z in range(NZ):
        both = got[z, RZ:].astype(F32)
        parts.append(both[:, :32] + both[:, 32:64])
        parts.append(both[:, 64:96] + both[:, 96:])
    remainder[...] = rhs_ext[...] - jnp.concatenate(parts, axis=0).T


def finish(got, rhs_ext):
    return pl.pallas_call(
        finish_kernel,
        out_shape=(
            jax.ShapeDtypeStruct((TILE, RHS), BF),
            jax.ShapeDtypeStruct((32, RHS), F32),
        ),
        compiler_params=pltpu.CompilerParams(vmem_limit_bytes=VMEM),
    )(got, rhs_ext)


def local(rhs_own, inverse, offdiag, pattern, rhs_ext):
    y, _, _, _ = coordinates()
    groups = [[NC * i + k for i in range(NZ)] for k in range(NC)]
    got = exchange(pick(pattern, offdiag), stride_groups())
    blob, btile = prep(offdiag, inverse, rhs_own)
    low = y < 2
    last = jnp.where(low, jnp.where(y == 0, got[5], got[2]), jnp.where(y == 2, got[0], got[7]))
    quad = jnp.stack(
        [
            jnp.where(low, got[0], got[4]),
            jnp.where(low, got[1], got[5]),
            jnp.where(low, got[4], got[6]),
            last,
        ]
    )
    line = lax.all_gather(quad, AXES, axis_index_groups=near_groups())
    blob, line = lax.optimization_barrier((blob, line))
    blobs = lax.all_gather(blob, "col")
    chunk = jnp.concatenate(
        [
            line[:2, 0],
            line[:2, 2],
            line[:2, 3],
            btile[None],
            line[2:, 0],
            line[2:, 2],
            line[:, 1],
        ],
        axis=0,
    )
    four = jnp.broadcast_to(chunk[None], (4, CHUNK, TILE, TILE))
    first = exchange(four, first_groups())
    right = move(first, ring_pairs(-1))
    left = move(first, ring_pairs(1))
    far_a = move(right[:2], ring_pairs(-1))
    far_b = move(left[2:], ring_pairs(1))
    pieces = [first, right, far_a, far_b, left]
    pieces += [move(p, swap_pairs()) for p in pieces]
    packed = solve(pattern, pieces, blobs.reshape(NZ * NC, BLOCKS, 2, 2, 32, TILE))
    home_again = lax.all_to_all(packed, "col", 0, 0, tiled=True, axis_index_groups=groups)
    return finish(home_again, rhs_ext)


def solution(mesh):
    return jax.shard_map(
        local,
        mesh=mesh,
        in_specs=(
            P(None, "row", None),
            P("col", None),
            P("row", "col"),
            P(None, "row"),
            P(("row", "col"), None),
        ),
        out_specs=(P("col", None), P(("row", "col"), None)),
        check_vma=False,
    )
```

```python
import jax
import jax.numpy as jnp
from jax import lax
from jax.experimental import pallas as pl
from jax.experimental.pallas import tpu as pltpu
from jax.sharding import PartitionSpec as P

AXES = ("row", "col")
NX, NY, NZ, NC = 4, 4, 16, 2
TILE = 128
SUPER = 8
TPS = 4
NZ_DEV = 6
OWN = 2
RHS = 512
RZ = RHS // NZ
CHUNK = 15
RHS_AT = 6
WAVES = ((0, 7), (7, 4), (11, 4))
INV0 = NZ_DEV * TILE
BLOB = INV0 + TPS * TILE
BLOCKS = NZ_DEV + TPS
F32 = jnp.float32
BF = jnp.bfloat16
VMEM = 60 * 1024 * 1024


def dev(y, x, z, k):
    return ((y % NY) * NX + x % NX) * (NZ * NC) + (z % NZ) * NC + k % NC


def every():
    for y in range(NY):
        for x in range(NX):
            for z in range(NZ):
                for k in range(NC):
                    yield y, x, z, k


def home(slot, y, z):
    first, second, third, fourth = (0, 1, 7, 8), (11, 12, 13, 14), (2, 3, 9, 10), (4, 5)
    if slot == 0:
        if y == 1:
            return 2, fourth[z]
        return 3 - y, (third + fourth)[z]
    if z < 8:
        return y, (first + second)[z]
    if y == 1:
        return y, fourth[z - 8]
    return y, (third + fourth)[z - 8]


def stride_groups():
    return [
        [dev(y, x, m + 4 * q, k) for y in pair for q in range(4)]
        for x in range(NX)
        for k in range(NC)
        for pair in ((0, 3), (1, 2))
        for m in range(4)
    ]


def near_groups():
    return [
        [dev(y, x, 4 * q + m, k) for m in range(4)]
        for y in range(NY)
        for x in range(NX)
        for k in range(NC)
        for q in range(4)
    ]


def first_groups():
    groups = []
    for z in range(NZ):
        for k in range(NC):
            for a in range(4):
                groups.append([dev(a, b, z, k) if k == 0 else dev(b, a, z, k) for b in range(4)])
    return groups


def ring_pairs(step):
    return [
        (dev(y, x, z, k), dev(y + step, x, z, k) if k == 0 else dev(y, x + step, z, k))
        for y, x, z, k in every()
    ]


def swap_pairs():
    return [(dev(y, x, z, k), dev(y, x, z, 1 - k)) for y, x, z, k in every()]


def move(value, pairs):
    return lax.ppermute(value, AXES, pairs)


def exchange(value, groups):
    return lax.all_to_all(value, AXES, 0, 0, tiled=True, axis_index_groups=groups)


def nt(a, b):
    return lax.dot_general(a, b, (((1,), (1,)), ((), ())), preferred_element_type=F32)


def coordinates():
    row, col = lax.axis_index("row"), lax.axis_index("col")
    return row >> 2, row & 3, col >> 1, col & 1


def pick_kernel(pattern, off, send):
    y, _, z, _ = coordinates()
    tiles = []
    for slot in range(OWN):
        tile = jnp.zeros((TILE, TILE), F32)
        for k in range(NZ_DEV):
            block = off[k * TILE : (k + 1) * TILE].astype(F32)
            tile = jnp.where(pattern[z >> 1, k] == slot, block, tile)
        tiles.append(tile)
    for half in range(2):
        tile = jnp.where((y >> 1) == half, tiles[1], tiles[0]).astype(BF)
        for q in range(4):
            send[half * 4 + q] = tile


def pick(pattern, off):
    vm = pl.BlockSpec(memory_space=pltpu.VMEM)
    return pl.pallas_call(
        pick_kernel,
        out_shape=jax.ShapeDtypeStruct((8, TILE, TILE), BF),
        in_specs=[pl.BlockSpec(memory_space=pltpu.SMEM), vm],
        out_specs=vm,
        compiler_params=pltpu.CompilerParams(vmem_limit_bytes=VMEM),
    )(pattern, off)


def prep_kernel(off, inv, rhs, blob, btile, flat):
    _, _, z, _ = coordinates()
    blob[:INV0] = off[...]
    for j in range(TPS):
        blob[INV0 + j * TILE : INV0 + (j + 1) * TILE] = inv[:, j * TILE : (j + 1) * TILE]
    start = pl.multiple_of(z * RZ, RZ)
    for slot in range(OWN):
        flat[...] = rhs[slot].T
        part = flat[pl.ds(start, RZ), :]
        high = part.astype(BF)
        btile[slot * 2 * RZ : slot * 2 * RZ + RZ] = high
        btile[slot * 2 * RZ + RZ : (slot + 1) * 2 * RZ] = (part - high.astype(F32)).astype(BF)


def prep(off, inv, rhs):
    vm = pl.BlockSpec(memory_space=pltpu.VMEM)
    return pl.pallas_call(
        prep_kernel,
        out_shape=(
            jax.ShapeDtypeStruct((BLOB, TILE), BF),
            jax.ShapeDtypeStruct((TILE, TILE), BF),
        ),
        in_specs=[vm, vm, vm],
        out_specs=(vm, vm),
        scratch_shapes=[pltpu.VMEM((RHS, TILE), F32)],
        compiler_params=pltpu.CompilerParams(vmem_limit_bytes=VMEM),
        cost_estimate=pl.CostEstimate(flops=1 << 20, bytes_accessed=4 << 20, transcendentals=0),
    )(off, inv, rhs)


PIECES = ((0, 4), (4, 4), (8, 2), (10, 2), (12, 4))


def solve_kernel(pattern, *refs):
    pieces = refs[:10]
    blobs, out, factor, invs, rows_ext, upd, ext, sol, *wsems, isems, esem = refs[10:]
    my_y, my_x, _, core = coordinates()

    def load(first, count, sems):
        return [
            pltpu.make_async_copy(
                pieces[h * 5 + p].at[:, pl.ds(first, count)],
                factor.at[h, pl.ds(at, blocks), pl.ds(first, count)],
                sems.at[h * 5 + p],
            )
            for h in range(2)
            for p, (at, blocks) in enumerate(PIECES)
        ]

    waves = [load(first, count, sems) for (first, count), sems in zip(WAVES, wsems)]
    ext_load = pltpu.make_async_copy(
        blobs.at[:, pl.ds(0, NZ_DEV), :, core], rows_ext, esem
    )
    inv_loads, inv_lows = [], []
    for s in range(SUPER):
        four = pl.ds(s * TPS, TPS)
        inv_loads.append(
            pltpu.make_async_copy(
                blobs.at[four, pl.ds(NZ_DEV, 2)], invs.at[four, pl.ds(0, 2)], isems.at[2 * s]
            )
        )
        lower = pl.ds(s * TPS + 2, 2)
        inv_lows.append(
            pltpu.make_async_copy(
                blobs.at[lower, pl.ds(NZ_DEV + 2, 2)],
                invs.at[lower, pl.ds(2, 2)],
                isems.at[2 * s + 1],
            )
        )
    for wave, inv_load, inv_low in zip(waves, inv_loads, inv_lows):
        for c in wave + [inv_load, inv_low]:
            c.start()
    for c in inv_loads[len(WAVES) :] + inv_lows[len(WAVES) :] + [ext_load]:
        c.start()
    upd[...] = jnp.zeros_like(upd)
    ext[...] = jnp.zeros_like(ext)
    def position(parity, y, x):
        if parity == 0:
            return ((y - my_y) & 3) * 4 + x
        return ((x - my_x) & 3) * 4 + y

    def block(parity, y, x, place):
        return factor[parity ^ core, position(parity, y, x), place]

    def rhs_tile(t):
        slot, y, x = t // 16, t % 16 // NX, t % NX
        where = jnp.where(core == 0, position(0, y, x), position(1, y, x))
        base = slot * 2 * RZ
        high = factor[0, where, RHS_AT, base : base + RZ].astype(F32)
        low = factor[0, where, RHS_AT, base + RZ : base + 2 * RZ].astype(F32)
        return high + low

    for s in range(SUPER):
        if s < len(WAVES):
            for c in waves[s]:
                c.wait()
        inv_loads[s].wait()
        inv_lows[s].wait()
        current = jnp.concatenate(
            [(rhs_tile(t) - upd[t]).astype(BF) for t in range(s * TPS, (s + 1) * TPS)], axis=1
        )
        solved = []
        for i in range(TPS):
            c = s * TPS + i
            rows = jnp.concatenate(
                [invs[c, j].reshape(TILE, TILE) for j in range(i + 1)], axis=1
            )
            x_i = nt(current[:, : (i + 1) * TILE], rows).astype(BF)
            sol[c] = x_i
            solved.append(x_i)
        x_s = jnp.concatenate(solved, axis=1)
        for t in range((s + 1) * TPS, SUPER * TPS, 2):
            rows = []
            for n in range(2):
                slot, y, x = (t + n) // 16, (t + n) % 16 // NX, (t + n) % NX
                parts = []
                for j in range(TPS):
                    at_y, place = home(slot, y, 2 * s + j // 2)
                    parts.append(block(j % 2, at_y, x, place))
                rows.append(jnp.concatenate(parts, axis=1))
            more = nt(x_s, jnp.concatenate(rows, axis=0))
            for n in range(2):
                upd[t + n] += more[:, n * TILE : (n + 1) * TILE]
    ext_load.wait()
    for s in range(SUPER):
        x_s = jnp.concatenate([sol[s * TPS + j] for j in range(TPS)], axis=1)
        for k in range(NZ_DEV):
            rows = jnp.concatenate(
                [rows_ext[s * TPS + j, k].reshape(64, TILE) for j in range(TPS)], axis=1
            )
            ext[pattern[s, k]] += nt(x_s, rows)
    for z in range(NZ):
        out[z, :RZ] = sol[2 * z + core]
        part = ext[OWN + z // 2][:, (z % 2) * 32 : (z % 2) * 32 + 32]
        high = part.astype(BF)
        low = (part - high.astype(F32)).astype(BF)
        both = jnp.concatenate([high, low], axis=1)
        out[z, RZ:] = jnp.concatenate([both[: RZ // 2], both[RZ // 2 :]], axis=1)


def solve(pattern, pieces, blobs):
    hbm = pl.BlockSpec(memory_space=pl.ANY)
    return pl.pallas_call(
        solve_kernel,
        out_shape=jax.ShapeDtypeStruct((NZ, RZ + RZ // 2, TILE), BF),
        in_specs=[pl.BlockSpec(memory_space=pltpu.SMEM)] + [hbm] * 11,
        out_specs=pl.BlockSpec(memory_space=pltpu.VMEM),
        scratch_shapes=[
            pltpu.VMEM((2, 16, CHUNK, TILE, TILE), BF),
            pltpu.VMEM((SUPER * TPS, TPS, 2, 2, 32, TILE), BF),
            pltpu.VMEM((SUPER * TPS, NZ_DEV, 2, 32, TILE), BF),
            pltpu.VMEM((SUPER * TPS, RZ, TILE), F32),
            pltpu.VMEM((10, RZ, 64), F32),
            pltpu.VMEM((SUPER * TPS, RZ, TILE), BF),
            pltpu.SemaphoreType.DMA((10,)),
            pltpu.SemaphoreType.DMA((10,)),
            pltpu.SemaphoreType.DMA((10,)),
            pltpu.SemaphoreType.DMA((2 * SUPER,)),
            pltpu.SemaphoreType.DMA,
        ],
        compiler_params=pltpu.CompilerParams(vmem_limit_bytes=VMEM),
    )(pattern, *pieces, blobs)


def finish_kernel(got, rhs_ext, solution, remainder):
    x = jnp.concatenate([got[z, :RZ].astype(F32) for z in range(NZ)], axis=0)
    solution[...] = x.T.astype(BF)
    parts = []
    for z in range(NZ):
        both = got[z, RZ:].astype(F32)
        parts.append(both[:, :32] + both[:, 32:64])
        parts.append(both[:, 64:96] + both[:, 96:])
    remainder[...] = rhs_ext[...] - jnp.concatenate(parts, axis=0).T


def finish(got, rhs_ext):
    return pl.pallas_call(
        finish_kernel,
        out_shape=(
            jax.ShapeDtypeStruct((TILE, RHS), BF),
            jax.ShapeDtypeStruct((32, RHS), F32),
        ),
        compiler_params=pltpu.CompilerParams(vmem_limit_bytes=VMEM),
    )(got, rhs_ext)


def local(rhs_own, inverse, offdiag, pattern, rhs_ext):
    y, _, _, _ = coordinates()
    groups = [[NC * i + k for i in range(NZ)] for k in range(NC)]
    got = exchange(pick(pattern, offdiag), stride_groups())
    blob, btile = prep(offdiag, inverse, rhs_own)
    low = y < 2
    last = jnp.where(low, jnp.where(y == 0, got[5], got[2]), jnp.where(y == 2, got[0], got[7]))
    quad = jnp.stack(
        [
            jnp.where(low, got[0], got[4]),
            jnp.where(low, got[1], got[5]),
            jnp.where(low, got[4], got[6]),
            last,
        ]
    )
    line = lax.all_gather(quad, AXES, axis_index_groups=near_groups())
    blob, line = lax.optimization_barrier((blob, line))
    blobs = lax.all_gather(blob, "col")
    chunk = jnp.concatenate(
        [
            line[:2, 0],
            line[:2, 2],
            line[:2, 3],
            btile[None],
            line[2:, 0],
            line[2:, 2],
            line[:, 1],
        ],
        axis=0,
    )
    four = jnp.broadcast_to(chunk[None], (4, CHUNK, TILE, TILE))
    first = exchange(four, first_groups())
    right = move(first, ring_pairs(-1))
    left = move(first, ring_pairs(1))
    far_a = move(right[:2], ring_pairs(-1))
    far_b = move(left[2:], ring_pairs(1))
    pieces = [first, right, far_a, far_b, left]
    pieces += [move(p, swap_pairs()) for p in pieces]
    packed = solve(pattern, pieces, blobs.reshape(NZ * NC, BLOCKS, 2, 2, 32, TILE))
    home_again = lax.all_to_all(packed, "col", 0, 0, tiled=True, axis_index_groups=groups)
    return finish(home_again, rhs_ext)


def solution(mesh):
    return jax.shard_map(
        local,
        mesh=mesh,
        in_specs=(
            P(None, "row", None),
            P("col", None),
            P("row", "col"),
            P(None, "row"),
            P(("row", "col"), None),
        ),
        out_specs=(P("col", None), P(("row", "col"), None)),
        check_vma=False,
    )
```
